32 devices in a mesh: grp: 2 (over y), fsdp: 8 (over z, x), seq: 2 (over core).
Axes of the slice: x: 2, y: 2, z: 4, core: 2. Of those that a mesh axis runs over, the one named last changes fastest.
Arguments:
- image_tokens: bfloat16 [16, 512, 3072], P(('grp', 'fsdp'), 'seq'), parts along dimension 0, may hold values from -6 to 6
- adjoint: bfloat16 [16, 512, 3072], P(('grp', 'fsdp'), 'seq'), parts along dimension 0, may hold values from -24 to 24
- attn_keys: bfloat16 [16, 768, 1536], P(('grp', 'fsdp'), 'seq'), parts along dimension 0, may hold values from -2.5 to 2.5
- attn_values: bfloat16 [16, 768, 1536], P(('grp', 'fsdp'), 'seq'), parts along dimension 0, may hold values from -6 to 6
- w_query: bfloat16 [3072, 1536], P('fsdp', 'seq'), may hold values from -0.109375 to 0.109375
- w_out: bfloat16 [1536, 3072], P('seq', 'fsdp'), may hold values from -0.15625 to 0.15625
- q_gain: float32 [128], replicated, may hold values from 1 to 2.5
- mod_table: float32 [28, 3, 3072], replicated, may hold values from -4 to 4
- timesteps: int32 [16], P(('grp', 'fsdp')), parts along dimension 0, may hold values from 0 to 27
- text_counts: int32 [16], P(('grp', 'fsdp')), parts along dimension 0, may hold values from 1 to 256
Outputs:
- branch_cotangent: float32 [16, 512, 3072], P(('grp', 'fsdp'), 'seq'), parts along dimension 0
The draws below stay inside these ranges and needn't reach their ends.
There are 2 independent parts, one for each index of `grp`. The reference program is written for one: setup_inputs(seed, part) draws one part's arguments, and reference() takes and returns one part's arrays. A program takes and returns all parts, laid end to end along the dimension named above; an argument that names none is the same for every part. Nothing has to cross between parts.
Inputs may be any that keep to these rules, and one draw needn't show every extreme that they name: Of a prompt's 256 text keys, the first text_counts of them are real and the rest are padding.
All inputs are finite; a program needn't handle non-finite values.
Results may differ from the reference program's by a relative error of at most 0.0092.
Values may be sent and summed in bfloat16 or wider, within the bound.
A program may use at most 128 MiB of HBM per device.

```python
import math
import jax
import jax.numpy as jnp
from jax import lax

D = 3072
HD = 128
TSTEPS = 28
HW = 1536
IMG = 512
TXT = 256
KEYS = 768
PROMPTS = 8


def touch_ends(array, own_key, smallest, largest):
    longest = array.shape.index(max(array.shape))
    spots = []
    for shift in (0, 1):
        where = [jax.random.randint(jax.random.fold_in(own_key, axis), (), 0, length) for axis, length in enumerate(array.shape)]
        where[longest] = (where[longest] + shift) % array.shape[longest]
        spots.append(tuple(where))
    return array.at[spots[0]].set(smallest).at[spots[1]].set(largest)


def steps_of(stream_key, shape, cuts, low, top_value):
    loudness, own = 1.0, jax.random.fold_in(stream_key, 6)
    for dim, parts in cuts:
        draws = jnp.exp(jax.random.uniform(jax.random.fold_in(own, dim), (parts,), jnp.float32, low / len(cuts), top_value / len(cuts)))
        loudness = loudness * jnp.repeat(draws, shape[dim] // parts).reshape([-1 if axis == dim else 1 for axis in range(len(shape))])
    return loudness


def normal_values(rng, extent, spread, bound, cuts=(), kind=jnp.bfloat16):
    factor_of = steps_of(rng, extent, cuts, -0.22, 0.18) if cuts else 1.0
    entries = jax.random.normal(rng, extent, jnp.float32) * spread * factor_of
    return jnp.minimum(jnp.maximum(entries, -bound), bound).astype(kind)


def setup_inputs(seed: int = 0, part: int = 0) -> dict:
    arg_keys = jax.random.split(jax.random.key(seed), 11)
    part_splits = jax.random.split(jax.random.fold_in(arg_keys[10], part), 11)
    return {
        "image_tokens": normal_values(part_splits[0], (PROMPTS, IMG, D), 1.0, 6.0, ((0, 8), (1, 2))),
        "adjoint": normal_values(part_splits[1], (PROMPTS, IMG, D), 4.0, 24.0, ((0, 8), (1, 2))),
        "attn_keys": normal_values(part_splits[2], (PROMPTS, KEYS, HW), 1.0, 2.5, ((0, 8), (1, 2))),
        "attn_values": normal_values(part_splits[3], (PROMPTS, KEYS, HW), 1.0, 6.0, ((0, 8), (1, 2))),
        "w_query": normal_values(arg_keys[4], (D, HW), D ** -0.5, 0.109375, ((0, 8), (1, 2))),
        "w_out": normal_values(arg_keys[5], (HW, D), HW ** -0.5, 0.15625, ((0, 2), (1, 8))),
        "q_gain": jnp.clip(jnp.exp(jax.random.uniform(arg_keys[6], (HD,), jnp.float32, math.log(1.0), math.log(2.5))), 1.0, 2.5),
        "mod_table": normal_values(arg_keys[7], (TSTEPS, 3, D), 1.0, 4.0, (), jnp.float32),
        "timesteps": touch_ends(jax.random.randint(part_splits[8], (PROMPTS,), 0, TSTEPS), jax.random.fold_in(part_splits[8], 1), 0, TSTEPS - 1).astype(jnp.int32),
        "text_counts": touch_ends(jax.random.randint(part_splits[9], (PROMPTS,), 1, TXT + 1), jax.random.fold_in(part_splits[9], 1), 1, TXT).astype(jnp.int32),
    }


def contract_last(left, right):
    return lax.dot_general(left, right, (((1,), (1,)), ((), ())), preferred_element_type=jnp.float32)

def modulate(tokens_in, shift_row, scale_row):
    row_mean = lax.optimization_barrier(jnp.mean(tokens_in, axis=-1, keepdims=True))
    centred = tokens_in - row_mean
    variance = lax.optimization_barrier(jnp.mean(centred * centred, axis=-1, keepdims=True))
    return centred * lax.rsqrt(variance + 1e-06) * (1.0 + scale_row) + shift_row

def head_norm(query, gain_vec):
    row_count = query.shape[0]
    grouped = query.reshape(row_count, -1, gain_vec.shape[0])
    square_mean = lax.optimization_barrier(jnp.mean(grouped * grouped, axis=-1, keepdims=True))
    return (grouped * lax.rsqrt(square_mean + 1e-06) * gain_vec).reshape(row_count, -1)

def attend(q_normed, key_rows, value_rows, grad_out, usable, head_dim):
    row_count = q_normed.shape[0]
    key_count = key_rows.shape[0]
    head_count = q_normed.shape[1] // head_dim
    factor = head_dim ** (-0.5)

    def split_heads(matrix, length):
        return matrix.reshape(length, head_count, head_dim).transpose(1, 0, 2)

    def one_head(pieces):
        query_head, key_head, value_head, grad_head = pieces
        scores = contract_last(query_head, key_head) * factor
        exp_terms = jnp.where(usable[None, :], jnp.exp(scores), 0.0)
        attn_probs = exp_terms / lax.optimization_barrier(jnp.sum(exp_terms, axis=-1, keepdims=True))
        d_probs = contract_last(grad_head, value_head)
        centre = lax.optimization_barrier(jnp.sum(attn_probs * d_probs, axis=-1, keepdims=True))
        d_scores = (attn_probs * (d_probs - centre) * factor).astype(jnp.bfloat16)
        return jnp.dot(d_scores, key_head, preferred_element_type=jnp.float32)
    result = lax.map(one_head, (split_heads(q_normed, row_count), split_heads(key_rows, key_count), split_heads(value_rows, key_count), split_heads(grad_out, row_count)))
    return result.transpose(1, 0, 2).reshape(row_count, head_count * head_dim)

def reference(image_tokens, adjoint, attn_keys, attn_values, w_query, w_out, q_gain, mod_table, timesteps, text_counts):
    positions = jnp.arange(KEYS, dtype=jnp.int32)

    def one_prompt(pieces):
        tokens, grad_in, key_rows, value_rows, step_index, text_count = pieces
        modulation = lax.dynamic_index_in_dim(mod_table, step_index, 0, keepdims=False)
        shift_row, scale_row, gate_row = (modulation[0], modulation[1], modulation[2])
        tokens_f = tokens.astype(jnp.float32)
        normed_f, norm_pull = jax.vjp(lambda tokens_in: modulate(tokens_in, shift_row, scale_row), tokens_f)
        normed = normed_f.astype(jnp.bfloat16)
        query = jnp.dot(normed, w_query, preferred_element_type=jnp.float32)
        q_normed_f, query_pull = jax.vjp(lambda query_in: head_norm(query_in, q_gain), query)
        q_normed = q_normed_f.astype(jnp.bfloat16)
        d_branch = (gate_row * grad_in.astype(jnp.float32)).astype(jnp.bfloat16)
        d_attn = contract_last(d_branch, w_out).astype(jnp.bfloat16)
        usable = (positions >= TXT) | (positions < text_count)
        d_qnormed = attend(q_normed, key_rows, value_rows, d_attn, usable, HD)
        d_query = query_pull(d_qnormed)[0].astype(jnp.bfloat16)
        d_normed = contract_last(d_query, w_query)
        return norm_pull(d_normed)[0]
    return lax.map(one_prompt, (image_tokens, adjoint, attn_keys, attn_values, timesteps, text_counts))
```

```python
import jax
import jax.numpy as jnp
from jax import lax
from jax.sharding import PartitionSpec as P

HD = 128
SWAP = ((0, 1), (1, 0))


def contract_last(left, right):
    return lax.dot_general(
        left, right, (((1,), (1,)), ((), ())), preferred_element_type=jnp.float32
    )


def swap(piece):
    return lax.ppermute(piece, "seq", SWAP)


def local(
    image_tokens,
    adjoint,
    attn_keys,
    attn_values,
    w_query,
    w_out,
    q_gain,
    mod_table,
    timesteps,
    text_counts,
):
    me = lax.axis_index("seq")
    half = w_query.shape[1]
    heads = half // HD
    factor = HD**-0.5
    w_q = lax.all_gather(w_query, "fsdp", axis=0, tiled=True)
    w_o = lax.all_gather(w_out.T, "fsdp", axis=0, tiled=True)

    modulation = lax.dynamic_index_in_dim(mod_table, timesteps[0], 0, keepdims=False)
    shift_row, scale_row, gate_row = (modulation[0], modulation[1], modulation[2])
    tokens = image_tokens[0].astype(jnp.float32)
    mean = jnp.mean(tokens, axis=-1, keepdims=True)
    centred = tokens - mean
    inv = lax.rsqrt(jnp.mean(centred * centred, axis=-1, keepdims=True) + 1e-06)
    normed = (centred * inv * (1.0 + scale_row) + shift_row).astype(jnp.bfloat16)
    d_branch = (gate_row * adjoint[0].astype(jnp.float32)).astype(jnp.bfloat16)

    def halves(rows):
        own = lax.dynamic_slice_in_dim(rows, me * half, half, 1)
        other = lax.dynamic_slice_in_dim(rows, (1 - me) * half, half, 1)
        return jnp.concatenate([own, swap(other)], axis=0)

    keys, values = halves(attn_keys[0]), halves(attn_values[0])
    key_rows = attn_keys.shape[1]
    txt = keys.shape[0] // 3
    spots = jnp.arange(key_rows, dtype=jnp.int32)
    positions = jnp.concatenate([me * key_rows + spots, (1 - me) * key_rows + spots])
    usable = (positions >= txt) | (positions < text_counts[0])

    normed_all = jnp.concatenate([normed, swap(normed)], axis=0)
    d_branch_all = jnp.concatenate([d_branch, swap(d_branch)], axis=0)
    query = jnp.dot(normed_all, w_q, preferred_element_type=jnp.float32)
    d_attn = jnp.dot(d_branch_all, w_o, preferred_element_type=jnp.float32).astype(jnp.bfloat16)
    parts = []
    for head in range(heads):
        cols = slice(head * HD, (head + 1) * HD)
        q_head, k_head, v_head = query[:, cols], keys[:, cols], values[:, cols]
        root = lax.rsqrt(jnp.mean(q_head * q_head, axis=-1, keepdims=True) + 1e-06)
        unit = q_head * root
        q_normed = (unit * q_gain).astype(jnp.bfloat16)
        scores = contract_last(q_normed, k_head) * factor
        terms = jnp.where(usable[None, :], jnp.exp(scores), 0.0)
        probs = terms / jnp.sum(terms, axis=-1, keepdims=True)
        d_probs = contract_last(d_attn[:, cols], v_head)
        centre = jnp.sum(probs * d_probs, axis=-1, keepdims=True)
        d_scores = (probs * (d_probs - centre) * factor).astype(jnp.bfloat16)
        d_unit = jnp.dot(d_scores, k_head, preferred_element_type=jnp.float32) * q_gain
        d_query = root * (d_unit - unit * jnp.mean(d_unit * unit, axis=-1, keepdims=True))
        parts.append(d_query.astype(jnp.bfloat16))
    d_query = jnp.concatenate(parts, axis=1)
    count = tokens.shape[0]
    theirs = contract_last(d_query[count:], w_q).astype(jnp.bfloat16)
    mine = contract_last(d_query[:count], w_q)
    d_normed = mine + swap(theirs).astype(jnp.float32)
    d_hat = d_normed * (1.0 + scale_row)
    hat = centred * inv
    d_mean = jnp.mean(d_hat, axis=-1, keepdims=True)
    d_proj = jnp.mean(d_hat * hat, axis=-1, keepdims=True)
    return (inv * (d_hat - d_mean - hat * d_proj))[None]


def solution(mesh):
    in_specs = (
        P(("grp", "fsdp"), "seq", None),
        P(("grp", "fsdp"), "seq", None),
        P(("grp", "fsdp"), "seq", None),
        P(("grp", "fsdp"), "seq", None),
        P("fsdp", "seq"),
        P("seq", "fsdp"),
        P(),
        P(),
        P(("grp", "fsdp")),
        P(("grp", "fsdp")),
    )
    out_specs = P(("grp", "fsdp"), "seq", None)
    return jax.shard_map(local, mesh=mesh, in_specs=in_specs, out_specs=out_specs, check_vma=False)
```

```python
import functools
import jax
import jax.numpy as jnp
from jax import lax
from jax.experimental import pallas as pl
from jax.experimental.pallas import tpu as pltpu
from jax.sharding import PartitionSpec as P

HD = 128
BF, F32 = jnp.bfloat16, jnp.float32
ROWS = 64
MESH = pl.DeviceIdType.MESH


def contract_last(left, right):
    return lax.dot_general(left, right, (((1,), (1,)), ((), ())), preferred_element_type=F32)


def kernel(
    Z, X,
    tok_ref, adj_ref, key_ref, val_ref, wq_ref, wo_ref, mod_ref, mask_ref, gain_ref,
    out_ref,
    wq, wo, normed, branch, keys, values, query, probs, dattn, dquery, theirs, theirs_in, total,
    recv_sem, send_sem, pair_recv, pair_send, tile_recv, tile_send,
):
    F = Z * X
    S, half = wq_ref.shape
    D = tok_ref.shape[1]
    rows, key_rows = tok_ref.shape[0], key_ref.shape[0]
    heads = half // HD
    factor = HD**-0.5
    g, me, c = lax.axis_index("grp"), lax.axis_index("fsdp"), lax.axis_index("seq")
    z, x = me // X, me % X
    near = [
        (z > 0, {"fsdp": me - X}),
        (z < Z - 1, {"fsdp": me + X}),
        (x > 0, {"fsdp": me - 1}),
        (x < X - 1, {"fsdp": me + 1}),
    ]
    twin, pair = {"grp": 1 - g}, {"seq": 1 - c}

    barrier = pltpu.get_barrier_semaphore()
    for ok, dev in near:
        @pl.when(ok)
        def _(dev=dev):
            pl.semaphore_signal(barrier, inc=1, device_id=dev, device_id_type=MESH)
    pl.semaphore_signal(barrier, inc=1, device_id=twin, device_id_type=MESH)
    pl.semaphore_signal(barrier, inc=1, device_id=pair, device_id_type=MESH)
    present = sum(ok.astype(jnp.int32) for ok, _ in near)
    pl.semaphore_wait(barrier, present + 2)

    bufs = (wq, wo)
    mid = half // 2
    big = (mid // 2 + HD - 1) // HD * HD
    small = mid - big
    M = (g * mid, mid)
    T = ((1 - g) * mid, big)
    Q = (g * mid + big, small)
    N = ((1 - g) * mid, mid)
    U = ((1 - g) * mid + big, small)
    sent = []

    def piece(w, f, span):
        start = pl.multiple_of(f * S, 16)
        return bufs[w].at[pl.ds(start, S), pl.ds(pl.multiple_of(span[0], HD), span[1])]

    def copy(w, f, span, kind, way, dev):
        return pltpu.make_async_remote_copy(
            src_ref=piece(w, f, span), dst_ref=piece(w, f, span),
            send_sem=send_sem.at[way, w, f], recv_sem=recv_sem.at[kind, w, f],
            device_id=dev, device_id_type=MESH,
        )

    def send(ok, *spec):
        sent.append((ok, spec))
        @pl.when(ok)
        def _():
            copy(*spec).start()

    def take(ok, w, f, span, kind):
        @pl.when(ok)
        def _():
            copy(w, f, span, kind, 0, twin).wait_recv()

    def to_x(ok, w, f):
        send(ok & near[2][0], w, f, M, 0, 4, near[2][1])
        send(ok & near[3][0], w, f, M, 0, 5, near[3][1])

    def own_start(w):
        for side in (0, 1):
            ok, dev = near[side]
            send(ok, w, me, M, 0, 2 * side, dev)
        to_x(z >= 0, w, me)
        for side in (0, 1):
            ok, dev = near[side]
            send(ok, w, me, T, 1, 2 * side + 1, dev)

    def z_round(w, d):
        for ok, zz, side in ((z >= d, z - d, 1), (z + d < Z, z + d, 0)):
            f = zz * X + x
            go, dev = near[side]
            take(ok, w, f, M, 0)
            send(ok & go, w, f, M, 0, 2 * side, dev)
            to_x(ok, w, f)
            send(ok, w, f, Q, 2, 6, twin)
            take(ok, w, f, T, 1)
            send(ok & go, w, f, T, 1, 2 * side + 1, dev)

    def planes(d):
        return [(z >= 0, z)] if d == 0 else [(z >= d, z - d), (z + d < Z, z + d)]

    def x_round(w, d):
        for okz, zz in planes(d):
            for e in range(1, X):
                for okx, xx, side in ((x >= e, x - e, 3), (x + e < X, x + e, 2)):
                    ok, f = okz & okx, zz * X + xx
                    go, dev = near[side]
                    take(ok, w, f, M, 0)
                    if X > 2:
                        send(ok & go, w, f, M, 0, 2 + side, dev)
                    send(ok, w, f, M, 1, 6, twin)

    def y_wait(w):
        for d in range(Z):
            for okz, zz in planes(d):
                if d:
                    take(okz, w, zz * X + x, U, 2)
                for e in range(1, X):
                    for okx, xx in ((x >= e, x - e), (x + e < X, x + e)):
                        take(okz & okx, w, zz * X + xx, N, 1)

    mine = pl.ds(pl.multiple_of(me * S, 16), S)
    wq[mine, :] = wq_ref[...]
    own_start(0)
    wo[mine, :] = wo_ref[...]
    own_start(1)

    def swap(src, dst, i):
        return pltpu.make_async_remote_copy(
            src_ref=src, dst_ref=dst, send_sem=pair_send.at[i], recv_sem=pair_recv.at[i],
            device_id=pair, device_id_type=MESH,
        )

    own_heads = pl.ds(pl.multiple_of(c * half, HD), half)
    other_heads = pl.ds(pl.multiple_of((1 - c) * half, HD), half)
    swaps = [
        swap(key_ref.at[:, other_heads], keys.at[pl.ds(key_rows, key_rows), :], 0),
        swap(val_ref.at[:, other_heads], values.at[pl.ds(key_rows, key_rows), :], 1),
    ]
    for s in swaps:
        s.start()

    def stats(r):
        tokens = tok_ref[r, :].astype(F32)
        centred = tokens - jnp.mean(tokens, axis=-1, keepdims=True)
        inv = lax.rsqrt(jnp.mean(centred * centred, axis=-1, keepdims=True) + 1e-06)
        return centred, inv

    def block(i, size):
        return pl.ds(pl.multiple_of(i * size, size), size)

    def prepare(i, carry):
        r = block(i, ROWS)
        centred, inv = stats(r)
        normed[r, :] = (centred * inv * (1.0 + mod_ref[1:2, :]) + mod_ref[0:1, :]).astype(BF)
        branch[r, :] = (mod_ref[2:3, :] * adj_ref[r, :].astype(F32)).astype(BF)
        return carry

    lax.fori_loop(0, rows // ROWS, prepare, 0)
    low, high = pl.ds(0, rows), pl.ds(rows, rows)
    swaps += [
        swap(normed.at[low, :], normed.at[high, :], 2),
        swap(branch.at[low, :], branch.at[high, :], 3),
    ]
    swaps[2].start()
    swaps[3].start()
    keys[pl.ds(0, key_rows), :] = key_ref[:, own_heads]
    values[pl.ds(0, key_rows), :] = val_ref[:, own_heads]

    def make_query():
        def step(i, carry):
            n = block(i, 256)
            query[:, n] = jnp.dot(normed[...], wq[:, n], preferred_element_type=F32)
            return carry
        lax.fori_loop(0, half // 256, step, 0)

    def unit_of(r, h):
        q = query[r, h]
        root = lax.rsqrt(jnp.mean(q * q, axis=-1, keepdims=True) + 1e-06)
        return q * root, root

    def soften(first, last):
        def step(i, carry):
            r, h = block(i % 2, rows), block(i // 2, HD)
            unit, _ = unit_of(r, h)
            scores = contract_last((unit * gain_ref[...]).astype(BF), keys[:, h]) * factor
            terms = jnp.where(mask_ref[...] > 0, jnp.exp(scores), 0.0)
            probs[i // 2, r, :] = terms * (1.0 / jnp.sum(terms, axis=-1, keepdims=True))
            return carry
        lax.fori_loop(2 * first, 2 * last, step, 0)

    for d in range(1, Z):
        z_round(0, d)
        x_round(0, d - 1)
    x_round(0, Z - 1)
    z_round(1, 1)
    x_round(1, 0)
    for s in swaps:
        s.wait()
    y_wait(0)
    make_query()
    z_round(1, 2)
    x_round(1, 1)
    soften(0, heads // 2)
    for d in range(3, Z):
        z_round(1, d)
        x_round(1, d - 1)
    soften(heads // 2, heads)
    x_round(1, Z - 1)
    y_wait(1)

    def make_dattn(i, carry):
        n = block(i, 256)
        dattn[:, n] = jnp.dot(branch[...], wo[:, n], preferred_element_type=F32).astype(BF)
        return carry
    lax.fori_loop(0, half // 256, make_dattn, 0)

    def back(i, carry):
        r, h = block(i % 2, rows), block(i // 2, HD)
        p = probs[i // 2, r, :]
        d_probs = contract_last(dattn[r, h], values[:, h])
        centre = jnp.sum(p * d_probs, axis=-1, keepdims=True)
        d_scores = (p * (d_probs - centre) * factor).astype(BF)
        d_unit = jnp.dot(d_scores, keys[:, h], preferred_element_type=F32) * gain_ref[...]
        unit, root = unit_of(r, h)
        inner = jnp.mean(d_unit * unit, axis=-1, keepdims=True)
        dquery[r, h] = (root * (d_unit - unit * inner)).astype(BF)
        return carry
    lax.fori_loop(0, 2 * heads, back, 0)

    wide = 512
    tiles = D // wide

    def tile_copy(i):
        n = block(i, wide)
        return pltpu.make_async_remote_copy(
            src_ref=theirs.at[:, n], dst_ref=theirs_in.at[:, n],
            send_sem=tile_send.at[i], recv_sem=tile_recv.at[i],
            device_id=pair, device_id_type=MESH,
        )

    def give(i, carry):
        n = block(i, wide)
        theirs[:, n] = contract_last(dquery[high, :], wq[n, :]).astype(BF)
        tile_copy(i).start()
        return carry
    lax.fori_loop(0, tiles, give, 0)

    def keep(i, carry):
        n = block(i, wide)
        total[:, n] = contract_last(dquery[low, :], wq[n, :])
        return carry
    lax.fori_loop(0, tiles, keep, 0)

    def settle(i, carry):
        tile_copy(i).wait()
        return carry
    lax.fori_loop(0, tiles, settle, 0)

    def finish(i, carry):
        r = block(i, ROWS)
        centred, inv = stats(r)
        hat = centred * inv
        d_hat = (total[r, :] + theirs_in[r, :].astype(F32)) * (1.0 + mod_ref[1:2, :])
        d_mean = jnp.mean(d_hat, axis=-1, keepdims=True)
        d_proj = jnp.mean(d_hat * hat, axis=-1, keepdims=True)
        out_ref[r, :] = inv * (d_hat - d_mean - hat * d_proj)
        return carry
    lax.fori_loop(0, rows // ROWS, finish, 0)

    for ok, spec in sent:
        @pl.when(ok)
        def _(spec=spec):
            copy(*spec).wait_send()


def local(
    fsdp,
    image_tokens,
    adjoint,
    attn_keys,
    attn_values,
    w_query,
    w_out,
    q_gain,
    mod_table,
    timesteps,
    text_counts,
):
    X = 2 ** ((fsdp.bit_length() - 1) // 3)
    while fsdp % X:
        X -= 1
    c = lax.axis_index("seq")
    _, rows, D = image_tokens.shape
    S, half = w_query.shape
    key_rows = attn_keys.shape[1]
    modulation = lax.dynamic_index_in_dim(mod_table, timesteps[0], 0, keepdims=False)
    spots = jnp.arange(key_rows, dtype=jnp.int32)
    positions = jnp.concatenate([c * key_rows + spots, (1 - c) * key_rows + spots])
    usable = (positions >= 2 * key_rows // 3) | (positions < text_counts[0])
    vmem = pl.BlockSpec(memory_space=pltpu.VMEM)
    heads = half // HD
    out = pl.pallas_call(
        functools.partial(kernel, fsdp // X, X),
        out_shape=jax.ShapeDtypeStruct((rows, D), F32),
        in_specs=[vmem] * 9,
        out_specs=vmem,
        scratch_shapes=[
            pltpu.VMEM((fsdp * S, half), BF),
            pltpu.VMEM((fsdp * S, half), BF),
            pltpu.VMEM((2 * rows, D), BF),
            pltpu.VMEM((2 * rows, D), BF),
            pltpu.VMEM((2 * key_rows, half), BF),
            pltpu.VMEM((2 * key_rows, half), BF),
            pltpu.VMEM((2 * rows, half), F32),
            pltpu.VMEM((heads, 2 * rows, 2 * key_rows), F32),
            pltpu.VMEM((2 * rows, half), BF),
            pltpu.VMEM((2 * rows, half), BF),
            pltpu.VMEM((rows, D), BF),
            pltpu.VMEM((rows, D), BF),
            pltpu.VMEM((rows, D), F32),
            pltpu.SemaphoreType.DMA((3, 2, fsdp)),
            pltpu.SemaphoreType.DMA((7, 2, fsdp)),
            pltpu.SemaphoreType.DMA((4,)),
            pltpu.SemaphoreType.DMA((4,)),
            pltpu.SemaphoreType.DMA((D // 512,)),
            pltpu.SemaphoreType.DMA((D // 512,)),
        ],
        compiler_params=pltpu.CompilerParams(
            collective_id=0, has_side_effects=True, vmem_limit_bytes=58 * 2**20
        ),
    )(
        image_tokens[0], adjoint[0], attn_keys[0], attn_values[0], w_query, w_out.T,
        modulation, usable.astype(F32)[None], q_gain[None],
    )
    return out[None]


def solution(mesh):
    in_specs = (
        P(("grp", "fsdp"), "seq", None),
        P(("grp", "fsdp"), "seq", None),
        P(("grp", "fsdp"), "seq", None),
        P(("grp", "fsdp"), "seq", None),
        P("fsdp", "seq"),
        P("seq", "fsdp"),
        P(),
        P(),
        P(("grp", "fsdp")),
        P(("grp", "fsdp")),
    )
    out_specs = P(("grp", "fsdp"), "seq", None)
    return jax.shard_map(
        functools.partial(local, mesh.shape["fsdp"]),
        mesh=mesh, in_specs=in_specs, out_specs=out_specs, check_vma=False,
    )
```

```python
import functools
import jax
import jax.numpy as jnp
from jax import lax
from jax.experimental import pallas as pl
from jax.experimental.pallas import tpu as pltpu
from jax.sharding import PartitionSpec as P

HD = 128
BF, F32 = jnp.bfloat16, jnp.float32
ROWS = 64
MESH = pl.DeviceIdType.MESH


def contract_last(left, right):
    return lax.dot_general(left, right, (((1,), (1,)), ((), ())), preferred_element_type=F32)


def kernel(
    Z, X,
    tok_ref, adj_ref, key_ref, val_ref, wq_ref, wo_ref, mod_ref, mask_ref, gain_ref,
    out_ref,
    wq, wo, normed, branch, keys, values, query, probs, dattn, dquery, theirs, theirs_in, total,
    recv_sem, send_sem, pair_recv, pair_send, tile_recv, tile_send,
):
    F = Z * X
    S, half = wq_ref.shape
    D = tok_ref.shape[1]
    rows, key_rows = tok_ref.shape[0], key_ref.shape[0]
    heads = half // HD
    factor = HD**-0.5
    g, me, c = lax.axis_index("grp"), lax.axis_index("fsdp"), lax.axis_index("seq")
    z, x = me // X, me % X
    near = [
        (z > 0, {"fsdp": me - X}),
        (z < Z - 1, {"fsdp": me + X}),
        (x > 0, {"fsdp": me - 1}),
        (x < X - 1, {"fsdp": me + 1}),
    ]
    twin, pair = {"grp": 1 - g}, {"seq": 1 - c}

    barrier = pltpu.get_barrier_semaphore()
    for ok, dev in near:
        @pl.when(ok)
        def _(dev=dev):
            pl.semaphore_signal(barrier, inc=1, device_id=dev, device_id_type=MESH)
    pl.semaphore_signal(barrier, inc=1, device_id=twin, device_id_type=MESH)
    pl.semaphore_signal(barrier, inc=1, device_id=pair, device_id_type=MESH)
    present = sum(ok.astype(jnp.int32) for ok, _ in near)
    pl.semaphore_wait(barrier, present + 2)

    bufs = (wq, wo)
    mid = half // 2
    big = (mid // 2 + HD - 1) // HD * HD
    small = mid - big
    M = (g * mid, mid)
    T = ((1 - g) * mid, big)
    Q = (g * mid + big, small)
    N = ((1 - g) * mid, mid)
    U = ((1 - g) * mid + big, small)
    sent = []

    def piece(w, f, span):
        start = pl.multiple_of(f * S, 16)
        return bufs[w].at[pl.ds(start, S), pl.ds(pl.multiple_of(span[0], HD), span[1])]

    def copy(w, f, span, kind, way, dev):
        return pltpu.make_async_remote_copy(
            src_ref=piece(w, f, span), dst_ref=piece(w, f, span),
            send_sem=send_sem.at[way, w, f], recv_sem=recv_sem.at[kind, w, f],
            device_id=dev, device_id_type=MESH,
        )

    def send(ok, *spec):
        sent.append((ok, spec))
        @pl.when(ok)
        def _():
            copy(*spec).start()

    def take(ok, w, f, span, kind):
        @pl.when(ok)
        def _():
            copy(w, f, span, kind, 0, twin).wait_recv()

    def to_x(ok, w, f):
        send(ok & near[2][0], w, f, M, 0, 4, near[2][1])
        send(ok & near[3][0], w, f, M, 0, 5, near[3][1])

    def own_m(w):
        to_x(z >= 0, w, me)
        for side in (0, 1):
            ok, dev = near[side]
            send(ok, w, me, M, 0, 2 * side, dev)

    def own_t(w):
        for side in (0, 1):
            ok, dev = near[side]
            send(ok, w, me, T, 1, 2 * side + 1, dev)

    def z_m(w, d):
        for ok, zz, side in ((z >= d, z - d, 1), (z + d < Z, z + d, 0)):
            f = zz * X + x
            go, dev = near[side]
            take(ok, w, f, M, 0)
            send(ok & go, w, f, M, 0, 2 * side, dev)
            to_x(ok, w, f)

    def z_t(w, d):
        for ok, zz, side in ((z >= d, z - d, 1), (z + d < Z, z + d, 0)):
            f = zz * X + x
            go, dev = near[side]
            take(ok, w, f, T, 1)
            send(ok & go, w, f, T, 1, 2 * side + 1, dev)

    def y_q(w):
        for d in range(1, Z):
            for ok, zz in planes(d):
                send(ok, w, zz * X + x, Q, 2, 6, twin)

    def planes(d):
        return [(z >= 0, z)] if d == 0 else [(z >= d, z - d), (z + d < Z, z + d)]

    def x_round(w, d):
        for okz, zz in planes(d):
            for e in range(1, X):
                for okx, xx, side in ((x >= e, x - e, 3), (x + e < X, x + e, 2)):
                    ok, f = okz & okx, zz * X + xx
                    go, dev = near[side]
                    take(ok, w, f, M, 0)
                    if X > 2:
                        send(ok & go, w, f, M, 0, 2 + side, dev)
                    send(ok, w, f, M, 1, 6, twin)

    def y_wait(w):
        for d in range(Z):
            for okz, zz in planes(d):
                if d:
                    take(okz, w, zz * X + x, U, 2)
                for e in range(1, X):
                    for okx, xx in ((x >= e, x - e), (x + e < X, x + e)):
                        take(okz & okx, w, zz * X + xx, N, 1)

    mine = pl.ds(pl.multiple_of(me * S, 16), S)
    wq[mine, :] = wq_ref[...]
    own_m(0)
    wo[mine, :] = wo_ref[...]
    own_m(1)

    def swap(src, dst, i):
        return pltpu.make_async_remote_copy(
            src_ref=src, dst_ref=dst, send_sem=pair_send.at[i], recv_sem=pair_recv.at[i],
            device_id=pair, device_id_type=MESH,
        )

    own_heads = pl.ds(pl.multiple_of(c * half, HD), half)
    other_heads = pl.ds(pl.multiple_of((1 - c) * half, HD), half)
    swaps = [
        swap(key_ref.at[:, other_heads], keys.at[pl.ds(key_rows, key_rows), :], 0),
        swap(val_ref.at[:, other_heads], values.at[pl.ds(key_rows, key_rows), :], 1),
    ]
    for s in swaps:
        s.start()

    def stats(r):
        tokens = tok_ref[r, :].astype(F32)
        centred = tokens - jnp.mean(tokens, axis=-1, keepdims=True)
        inv = lax.rsqrt(jnp.mean(centred * centred, axis=-1, keepdims=True) + 1e-06)
        return centred, inv

    def block(i, size):
        return pl.ds(pl.multiple_of(i * size, size), size)

    def prepare(i, carry):
        r = block(i, ROWS)
        centred, inv = stats(r)
        normed[r, :] = (centred * inv * (1.0 + mod_ref[1:2, :]) + mod_ref[0:1, :]).astype(BF)
        branch[r, :] = (mod_ref[2:3, :] * adj_ref[r, :].astype(F32)).astype(BF)
        return carry

    lax.fori_loop(0, rows // ROWS, prepare, 0)
    low, high = pl.ds(0, rows), pl.ds(rows, rows)
    swaps += [
        swap(normed.at[low, :], normed.at[high, :], 2),
        swap(branch.at[low, :], branch.at[high, :], 3),
    ]
    swaps[2].start()
    swaps[3].start()
    keys[pl.ds(0, key_rows), :] = key_ref[:, own_heads]
    values[pl.ds(0, key_rows), :] = val_ref[:, own_heads]

    def columns(which):
        return pl.ds(pl.multiple_of(which * mid, HD), mid)

    def make_query(which):
        n = columns(which)
        def step(i, carry):
            r = block(i, rows)
            query[r, n] = jnp.dot(normed[r, :], wq[:, n], preferred_element_type=F32)
            return carry
        lax.fori_loop(0, 2, step, 0)

    def unit_of(r, h):
        q = query[r, h]
        root = lax.rsqrt(jnp.mean(q * q, axis=-1, keepdims=True) + 1e-06)
        return q * root, root

    def soften(which, part):
        head = which * (heads // 2) + part
        def step(i, carry):
            r, h = block(i, rows), block(head, HD)
            unit, _ = unit_of(r, h)
            scores = contract_last((unit * gain_ref[...]).astype(BF), keys[:, h]) * factor
            terms = jnp.where(mask_ref[...] > 0, jnp.exp(scores), 0.0)
            probs[head, r, :] = terms * (1.0 / jnp.sum(terms, axis=-1, keepdims=True))
            return carry
        lax.fori_loop(0, 2, step, 0)

    def make_dattn(which):
        n = columns(which)
        def step(i, carry):
            r = block(i, rows)
            dattn[r, n] = jnp.dot(branch[r, :], wo[:, n], preferred_element_type=F32).astype(BF)
            return carry
        lax.fori_loop(0, 2, step, 0)

    def back(which, part):
        head = which * (heads // 2) + part
        def step(i, carry):
            r, h = block(i, rows), block(head, HD)
            p = probs[head, r, :]
            d_probs = contract_last(dattn[r, h], values[:, h])
            centre = jnp.sum(p * d_probs, axis=-1, keepdims=True)
            d_scores = (p * (d_probs - centre) * factor).astype(BF)
            d_unit = jnp.dot(d_scores, keys[:, h], preferred_element_type=F32) * gain_ref[...]
            unit, root = unit_of(r, h)
            inner = jnp.mean(d_unit * unit, axis=-1, keepdims=True)
            dquery[r, h] = (root * (d_unit - unit * inner)).astype(BF)
            return carry
        lax.fori_loop(0, 2, step, 0)

    early, late = g, 1 - g
    work = [functools.partial(make_query, early)]
    work += [functools.partial(soften, early, i) for i in range(heads // 2)]
    work += [functools.partial(make_dattn, early)]
    work += [functools.partial(back, early, i) for i in range(heads // 2)]

    def some(n):
        for _ in range(min(n, len(work))):
            work.pop(0)()

    for d in range(1, Z):
        z_m(0, d)
        x_round(0, d - 1)
        z_m(1, d)
        x_round(1, d - 1)
        if d == max(Z - 2, 1):
            own_t(0)
            own_t(1)
    x_round(0, Z - 1)
    y_q(0)
    z_t(0, 1)
    x_round(1, Z - 1)
    y_q(1)
    for s in swaps:
        s.wait()
    z_t(1, 1)
    for d in range(2, Z):
        some(2)
        z_t(0, d)
        some(1)
        z_t(1, d)
    some(len(work))
    y_wait(0)
    make_query(late)
    for i in range(heads // 2):
        soften(late, i)
    y_wait(1)
    make_dattn(late)
    for i in range(heads // 2):
        back(late, i)

    wide = 512
    tiles = D // wide

    def tile_copy(i):
        n = block(i, wide)
        return pltpu.make_async_remote_copy(
            src_ref=theirs.at[:, n], dst_ref=theirs_in.at[:, n],
            send_sem=tile_send.at[i], recv_sem=tile_recv.at[i],
            device_id=pair, device_id_type=MESH,
        )

    def give(i, carry):
        n = block(i, wide)
        theirs[:, n] = contract_last(dquery[high, :], wq[n, :]).astype(BF)
        tile_copy(i).start()
        return carry
    lax.fori_loop(0, tiles, give, 0)

    def keep(i, carry):
        n = block(i, wide)
        total[:, n] = contract_last(dquery[low, :], wq[n, :])
        return carry
    lax.fori_loop(0, tiles, keep, 0)

    def settle(i, carry):
        tile_copy(i).wait()
        return carry
    lax.fori_loop(0, tiles, settle, 0)

    def finish(i, carry):
        r = block(i, ROWS)
        centred, inv = stats(r)
        hat = centred * inv
        d_hat = (total[r, :] + theirs_in[r, :].astype(F32)) * (1.0 + mod_ref[1:2, :])
        d_mean = jnp.mean(d_hat, axis=-1, keepdims=True)
        d_proj = jnp.mean(d_hat * hat, axis=-1, keepdims=True)
        out_ref[r, :] = inv * (d_hat - d_mean - hat * d_proj)
        return carry
    lax.fori_loop(0, rows // ROWS, finish, 0)

    for ok, spec in sent:
        @pl.when(ok)
        def _(spec=spec):
            copy(*spec).wait_send()


def local(
    fsdp,
    image_tokens,
    adjoint,
    attn_keys,
    attn_values,
    w_query,
    w_out,
    q_gain,
    mod_table,
    timesteps,
    text_counts,
):
    X = 2 ** ((fsdp.bit_length() - 1) // 3)
    while fsdp % X:
        X -= 1
    c = lax.axis_index("seq")
    _, rows, D = image_tokens.shape
    S, half = w_query.shape
    key_rows = attn_keys.shape[1]
    modulation = lax.dynamic_index_in_dim(mod_table, timesteps[0], 0, keepdims=False)
    spots = jnp.arange(key_rows, dtype=jnp.int32)
    positions = jnp.concatenate([c * key_rows + spots, (1 - c) * key_rows + spots])
    usable = (positions >= 2 * key_rows // 3) | (positions < text_counts[0])
    vmem = pl.BlockSpec(memory_space=pltpu.VMEM)
    heads = half // HD
    out = pl.pallas_call(
        functools.partial(kernel, fsdp // X, X),
        out_shape=jax.ShapeDtypeStruct((rows, D), F32),
        in_specs=[vmem] * 9,
        out_specs=vmem,
        scratch_shapes=[
            pltpu.VMEM((fsdp * S, half), BF),
            pltpu.VMEM((fsdp * S, half), BF),
            pltpu.VMEM((2 * rows, D), BF),
            pltpu.VMEM((2 * rows, D), BF),
            pltpu.VMEM((2 * key_rows, half), BF),
            pltpu.VMEM((2 * key_rows, half), BF),
            pltpu.VMEM((2 * rows, half), F32),
            pltpu.VMEM((heads, 2 * rows, 2 * key_rows), F32),
            pltpu.VMEM((2 * rows, half), BF),
            pltpu.VMEM((2 * rows, half), BF),
            pltpu.VMEM((rows, D), BF),
            pltpu.VMEM((rows, D), BF),
            pltpu.VMEM((rows, D), F32),
            pltpu.SemaphoreType.DMA((3, 2, fsdp)),
            pltpu.SemaphoreType.DMA((7, 2, fsdp)),
            pltpu.SemaphoreType.DMA((4,)),
            pltpu.SemaphoreType.DMA((4,)),
            pltpu.SemaphoreType.DMA((D // 512,)),
            pltpu.SemaphoreType.DMA((D // 512,)),
        ],
        compiler_params=pltpu.CompilerParams(
            collective_id=0, has_side_effects=True, vmem_limit_bytes=58 * 2**20
        ),
    )(
        image_tokens[0], adjoint[0], attn_keys[0], attn_values[0], w_query, w_out.T,
        modulation, usable.astype(F32)[None], q_gain[None],
    )
    return out[None]


def solution(mesh):
    in_specs = (
        P(("grp", "fsdp"), "seq", None),
        P(("grp", "fsdp"), "seq", None),
        P(("grp", "fsdp"), "seq", None),
        P(("grp", "fsdp"), "seq", None),
        P("fsdp", "seq"),
        P("seq", "fsdp"),
        P(),
        P(),
        P(("grp", "fsdp")),
        P(("grp", "fsdp")),
    )
    out_specs = P(("grp", "fsdp"), "seq", None)
    return jax.shard_map(
        functools.partial(local, mesh.shape["fsdp"]),
        mesh=mesh, in_specs=in_specs, out_specs=out_specs, check_vma=False,
    )
```

```python
import functools
import jax
import jax.numpy as jnp
from jax import lax
from jax.experimental import pallas as pl
from jax.experimental.pallas import tpu as pltpu
from jax.sharding import PartitionSpec as P

HD = 128
BF, F32 = jnp.bfloat16, jnp.float32
ROWS = 64
MESH = pl.DeviceIdType.MESH


def contract_last(left, right):
    return lax.dot_general(left, right, (((1,), (1,)), ((), ())), preferred_element_type=F32)


def kernel(
    Z, X,
    tok_hbm, adj_hbm, key_ref, val_ref, wq_ref, wo_ref, mod_ref, mask_ref, gain_ref,
    out_ref,
    wq, wo, normed, branch, keys, values, query, probs, dattn, dquery, theirs, theirs_in, total,
    tok_ref, adj_ref, load_sem,
    recv_sem, send_sem, pair_recv, pair_send, tile_recv, tile_send,
):
    F = Z * X
    S, half = wq_ref.shape
    D = tok_hbm.shape[1]
    rows, key_rows = tok_hbm.shape[0], key_ref.shape[0]
    heads = half // HD
    factor = HD**-0.5
    g, me, c = lax.axis_index("grp"), lax.axis_index("fsdp"), lax.axis_index("seq")
    z, x = me // X, me % X
    near = [
        (z > 0, {"fsdp": me - X}),
        (z < Z - 1, {"fsdp": me + X}),
        (x > 0, {"fsdp": me - 1}),
        (x < X - 1, {"fsdp": me + 1}),
    ]
    twin, pair = {"grp": 1 - g}, {"seq": 1 - c}

    barrier = pltpu.get_barrier_semaphore()
    for ok, dev in near:
        @pl.when(ok)
        def _(dev=dev):
            pl.semaphore_signal(barrier, inc=1, device_id=dev, device_id_type=MESH)
    pl.semaphore_signal(barrier, inc=1, device_id=twin, device_id_type=MESH)
    pl.semaphore_signal(barrier, inc=1, device_id=pair, device_id_type=MESH)
    present = sum(ok.astype(jnp.int32) for ok, _ in near)
    pl.semaphore_wait(barrier, present + 2)

    bufs = (wq, wo)
    mid = half // 2
    big = (mid // 2 + HD - 1) // HD * HD
    small = mid - big
    M = (g * mid, mid)
    T = ((1 - g) * mid, big)
    Q = (g * mid + big, small)
    N = ((1 - g) * mid, mid)
    U = ((1 - g) * mid + big, small)
    sent = []

    def piece(w, f, span):
        start = pl.multiple_of(f * S, 16)
        return bufs[w].at[pl.ds(start, S), pl.ds(pl.multiple_of(span[0], HD), span[1])]

    def copy(w, f, span, kind, way, dev):
        return pltpu.make_async_remote_copy(
            src_ref=piece(w, f, span), dst_ref=piece(w, f, span),
            send_sem=send_sem.at[way, w, f], recv_sem=recv_sem.at[kind, w, f],
            device_id=dev, device_id_type=MESH,
        )

    def send(ok, *spec):
        sent.append((ok, spec))
        @pl.when(ok)
        def _():
            copy(*spec).start()

    def take(ok, w, f, span, kind):
        @pl.when(ok)
        def _():
            copy(w, f, span, kind, 0, twin).wait_recv()

    def to_x(ok, w, f):
        send(ok & near[2][0], w, f, M, 0, 4, near[2][1])
        send(ok & near[3][0], w, f, M, 0, 5, near[3][1])

    def own_m(w):
        to_x(z >= 0, w, me)
        for side in (0, 1):
            ok, dev = near[side]
            send(ok, w, me, M, 0, 2 * side, dev)

    def own_t(w):
        for side in (0, 1):
            ok, dev = near[side]
            send(ok, w, me, T, 1, 2 * side + 1, dev)

    def z_m(w, d):
        for ok, zz, side in ((z >= d, z - d, 1), (z + d < Z, z + d, 0)):
            f = zz * X + x
            go, dev = near[side]
            take(ok, w, f, M, 0)
            send(ok & go, w, f, M, 0, 2 * side, dev)
            to_x(ok, w, f)

    def z_t(w, d):
        for ok, zz, side in ((z >= d, z - d, 1), (z + d < Z, z + d, 0)):
            f = zz * X + x
            go, dev = near[side]
            take(ok, w, f, T, 1)
            send(ok & go, w, f, T, 1, 2 * side + 1, dev)

    def y_q(w):
        for d in range(1, Z):
            for ok, zz in planes(d):
                send(ok, w, zz * X + x, Q, 2, 6, twin)

    def planes(d):
        return [(z >= 0, z)] if d == 0 else [(z >= d, z - d), (z + d < Z, z + d)]

    def x_round(w, d):
        for okz, zz in planes(d):
            for e in range(1, X):
                for okx, xx, side in ((x >= e, x - e, 3), (x + e < X, x + e, 2)):
                    ok, f = okz & okx, zz * X + xx
                    go, dev = near[side]
                    take(ok, w, f, M, 0)
                    if X > 2:
                        send(ok & go, w, f, M, 0, 2 + side, dev)
                    send(ok, w, f, M, 1, 6, twin)

    def y_wait(w):
        for d in range(Z):
            for okz, zz in planes(d):
                if d:
                    take(okz, w, zz * X + x, U, 2)
                for e in range(1, X):
                    for okx, xx in ((x >= e, x - e), (x + e < X, x + e)):
                        take(okz & okx, w, zz * X + xx, N, 1)

    mine = pl.ds(pl.multiple_of(me * S, 16), S)
    wq[mine, :] = wq_ref[...]
    own_m(0)
    loads = [
        pltpu.make_async_copy(tok_hbm, tok_ref, load_sem.at[0]),
        pltpu.make_async_copy(adj_hbm, adj_ref, load_sem.at[1]),
    ]
    for load in loads:
        load.start()
    wo[mine, :] = wo_ref[...].T
    own_m(1)

    def swap(src, dst, i):
        return pltpu.make_async_remote_copy(
            src_ref=src, dst_ref=dst, send_sem=pair_send.at[i], recv_sem=pair_recv.at[i],
            device_id=pair, device_id_type=MESH,
        )

    own_heads = pl.ds(pl.multiple_of(c * half, HD), half)
    other_heads = pl.ds(pl.multiple_of((1 - c) * half, HD), half)
    swaps = [
        swap(key_ref.at[:, other_heads], keys.at[pl.ds(key_rows, key_rows), :], 0),
        swap(val_ref.at[:, other_heads], values.at[pl.ds(key_rows, key_rows), :], 1),
    ]
    for s in swaps:
        s.start()

    def stats(r):
        tokens = tok_ref[r, :].astype(F32)
        centred = tokens - jnp.mean(tokens, axis=-1, keepdims=True)
        inv = lax.rsqrt(jnp.mean(centred * centred, axis=-1, keepdims=True) + 1e-06)
        return centred, inv

    def block(i, size):
        return pl.ds(pl.multiple_of(i * size, size), size)

    def prepare(i, carry):
        r = block(i, ROWS)
        centred, inv = stats(r)
        normed[r, :] = (centred * inv * (1.0 + mod_ref[1:2, :]) + mod_ref[0:1, :]).astype(BF)
        branch[r, :] = (mod_ref[2:3, :] * adj_ref[r, :].astype(F32)).astype(BF)
        return carry

    for load in loads:
        load.wait()
    lax.fori_loop(0, rows // ROWS, prepare, 0)
    low, high = pl.ds(0, rows), pl.ds(rows, rows)
    swaps += [
        swap(normed.at[low, :], normed.at[high, :], 2),
        swap(branch.at[low, :], branch.at[high, :], 3),
    ]
    swaps[2].start()
    swaps[3].start()
    keys[pl.ds(0, key_rows), :] = key_ref[:, own_heads]
    values[pl.ds(0, key_rows), :] = val_ref[:, own_heads]

    def columns(which):
        return pl.ds(pl.multiple_of(which * mid, HD), mid)

    def make_query(which):
        n = columns(which)
        def step(i, carry):
            r = block(i, rows)
            query[r, n] = jnp.dot(normed[r, :], wq[:, n], preferred_element_type=F32)
            return carry
        lax.fori_loop(0, 2, step, 0)

    def unit_of(r, h):
        q = query[r, h]
        root = lax.rsqrt(jnp.mean(q * q, axis=-1, keepdims=True) + 1e-06)
        return q * root, root

    def soften(which, part):
        head = which * (heads // 2) + part
        def step(i, carry):
            r, h = block(i, rows), block(head, HD)
            unit, _ = unit_of(r, h)
            scores = contract_last((unit * gain_ref[...]).astype(BF), keys[:, h]) * factor
            terms = jnp.where(mask_ref[...] > 0, jnp.exp(scores), 0.0)
            probs[head, r, :] = terms * (1.0 / jnp.sum(terms, axis=-1, keepdims=True))
            return carry
        lax.fori_loop(0, 2, step, 0)

    def make_dattn(which):
        n = columns(which)
        def step(i, carry):
            r = block(i, rows)
            dattn[r, n] = jnp.dot(branch[r, :], wo[:, n], preferred_element_type=F32).astype(BF)
            return carry
        lax.fori_loop(0, 2, step, 0)

    def back(which, part):
        head = which * (heads // 2) + part
        def step(i, carry):
            r, h = block(i, rows), block(head, HD)
            p = probs[head, r, :]
            d_probs = contract_last(dattn[r, h], values[:, h])
            centre = jnp.sum(p * d_probs, axis=-1, keepdims=True)
            d_scores = (p * (d_probs - centre) * factor).astype(BF)
            d_unit = jnp.dot(d_scores, keys[:, h], preferred_element_type=F32) * gain_ref[...]
            unit, root = unit_of(r, h)
            inner = jnp.mean(d_unit * unit, axis=-1, keepdims=True)
            dquery[r, h] = (root * (d_unit - unit * inner)).astype(BF)
            return carry
        lax.fori_loop(0, 2, step, 0)

    early, late = g, 1 - g
    work = [functools.partial(make_query, early)]
    work += [functools.partial(soften, early, i) for i in range(heads // 2)]
    work += [functools.partial(make_dattn, early)]
    work += [functools.partial(back, early, i) for i in range(heads // 2)]

    def some(n):
        for _ in range(min(n, len(work))):
            work.pop(0)()

    for d in range(1, Z):
        z_m(0, d)
        x_round(0, d - 1)
        z_m(1, d)
        x_round(1, d - 1)
        if d == max(Z - 2, 1):
            own_t(0)
            own_t(1)
    x_round(0, Z - 1)
    y_q(0)
    z_t(0, 1)
    x_round(1, Z - 1)
    y_q(1)
    for s in swaps:
        s.wait()
    z_t(1, 1)
    for d in range(2, Z):
        some(2)
        z_t(0, d)
        some(1)
        z_t(1, d)
    some(len(work))
    y_wait(0)
    make_query(late)
    for i in range(heads // 2):
        soften(late, i)
    y_wait(1)
    make_dattn(late)
    for i in range(heads // 2):
        back(late, i)

    wide = 512
    tiles = D // wide

    def tile_copy(i):
        n = block(i, wide)
        return pltpu.make_async_remote_copy(
            src_ref=theirs.at[:, n], dst_ref=theirs_in.at[:, n],
            send_sem=tile_send.at[i], recv_sem=tile_recv.at[i],
            device_id=pair, device_id_type=MESH,
        )

    def give(i, carry):
        n = block(i, wide)
        theirs[:, n] = contract_last(dquery[high, :], wq[n, :]).astype(BF)
        tile_copy(i).start()
        return carry
    lax.fori_loop(0, tiles, give, 0)

    def keep(i, carry):
        n = block(i, wide)
        total[:, n] = contract_last(dquery[low, :], wq[n, :])
        return carry
    lax.fori_loop(0, tiles, keep, 0)

    def settle(i, carry):
        tile_copy(i).wait()
        return carry
    lax.fori_loop(0, tiles, settle, 0)

    def finish(i, carry):
        r = block(i, ROWS)
        centred, inv = stats(r)
        hat = centred * inv
        d_hat = (total[r, :] + theirs_in[r, :].astype(F32)) * (1.0 + mod_ref[1:2, :])
        d_mean = jnp.mean(d_hat, axis=-1, keepdims=True)
        d_proj = jnp.mean(d_hat * hat, axis=-1, keepdims=True)
        out_ref[r, :] = inv * (d_hat - d_mean - hat * d_proj)
        return carry
    lax.fori_loop(0, rows // ROWS, finish, 0)

    for ok, spec in sent:
        @pl.when(ok)
        def _(spec=spec):
            copy(*spec).wait_send()


def local(
    fsdp,
    image_tokens,
    adjoint,
    attn_keys,
    attn_values,
    w_query,
    w_out,
    q_gain,
    mod_table,
    timesteps,
    text_counts,
):
    X = 2 ** ((fsdp.bit_length() - 1) // 3)
    while fsdp % X:
        X -= 1
    c = lax.axis_index("seq")
    _, rows, D = image_tokens.shape
    S, half = w_query.shape
    key_rows = attn_keys.shape[1]
    modulation = lax.dynamic_index_in_dim(mod_table, timesteps[0], 0, keepdims=False)
    spots = jnp.arange(key_rows, dtype=jnp.int32)
    positions = jnp.concatenate([c * key_rows + spots, (1 - c) * key_rows + spots])
    usable = (positions >= 2 * key_rows // 3) | (positions < text_counts[0])
    vmem = pl.BlockSpec(memory_space=pltpu.VMEM)
    heads = half // HD
    out = pl.pallas_call(
        functools.partial(kernel, fsdp // X, X),
        out_shape=jax.ShapeDtypeStruct((rows, D), F32),
        in_specs=[pl.BlockSpec(memory_space=pl.ANY)] * 2 + [vmem] * 7,
        out_specs=vmem,
        scratch_shapes=[
            pltpu.VMEM((fsdp * S, half), BF),
            pltpu.VMEM((fsdp * S, half), BF),
            pltpu.VMEM((2 * rows, D), BF),
            pltpu.VMEM((2 * rows, D), BF),
            pltpu.VMEM((2 * key_rows, half), BF),
            pltpu.VMEM((2 * key_rows, half), BF),
            pltpu.VMEM((2 * rows, half), F32),
            pltpu.VMEM((heads, 2 * rows, 2 * key_rows), F32),
            pltpu.VMEM((2 * rows, half), BF),
            pltpu.VMEM((2 * rows, half), BF),
            pltpu.VMEM((rows, D), BF),
            pltpu.VMEM((rows, D), BF),
            pltpu.VMEM((rows, D), F32),
            pltpu.VMEM((rows, D), BF),
            pltpu.VMEM((rows, D), BF),
            pltpu.SemaphoreType.DMA((2,)),
            pltpu.SemaphoreType.DMA((3, 2, fsdp)),
            pltpu.SemaphoreType.DMA((7, 2, fsdp)),
            pltpu.SemaphoreType.DMA((4,)),
            pltpu.SemaphoreType.DMA((4,)),
            pltpu.SemaphoreType.DMA((D // 512,)),
            pltpu.SemaphoreType.DMA((D // 512,)),
        ],
        compiler_params=pltpu.CompilerParams(
            collective_id=0, has_side_effects=True, vmem_limit_bytes=58 * 2**20
        ),
    )(
        image_tokens[0], adjoint[0], attn_keys[0], attn_values[0], w_query, w_out,
        modulation, usable.astype(F32)[None], q_gain[None],
    )
    return out[None]


def solution(mesh):
    in_specs = (
        P(("grp", "fsdp"), "seq", None),
        P(("grp", "fsdp"), "seq", None),
        P(("grp", "fsdp"), "seq", None),
        P(("grp", "fsdp"), "seq", None),
        P("fsdp", "seq"),
        P("seq", "fsdp"),
        P(),
        P(),
        P(("grp", "fsdp")),
        P(("grp", "fsdp")),
    )
    out_specs = P(("grp", "fsdp"), "seq", None)
    return jax.shard_map(
        functools.partial(local, mesh.shape["fsdp"]),
        mesh=mesh, in_specs=in_specs, out_specs=out_specs, check_vma=False,
    )
```
